512 devices in a mesh: row: 32 (over x_hi, y, core), col: 16 (over x_lo, z).
Axes of the slice: x: 4 (x_hi: 2, x_lo: 2; x = x_hi * 2 + x_lo), y: 8, z: 8, core: 2. Of those that a mesh axis runs over, the one named last changes fastest.
Arguments:
- click_tiles: bfloat16 [4096, 512, 512], P(('row', 'col')), may hold values from 0 to 20
- tile_coords: int32 [4096, 2], P(('row', 'col')), may hold values from 0 to 7, as said below
- tile_count: int32 [512], P(('row', 'col')), may hold values from 1 to 8, as said below
- prior_labels: float32 [64, 65536], P(None, ('row', 'col')), may hold values from 0.01 to 10
- seed_ids: int32 [16384], P(('row', 'col')), may hold values from 0 to 65535, as said below
- seed_class: int32 [16384], P(('row', 'col')), may hold values from 0 to 63
Outputs:
- query_labels: float32 [64, 65536], P(None, ('row', 'col'))
- url_labels: float32 [64, 65536], P(None, ('col', 'row'))
The draws below stay inside these ranges and needn't reach their ends.
Inputs may be any that keep to these rules, and one draw needn't show every extreme that they name: `tile_coords`: within each device's 8 slots the (local query block, local URL block) pairs are distinct, first column below 4, second below 8. `tile_count`: some device has all 8 slots live. `seed_ids`: seeds d * 32 to (d + 1) * 32 - 1 name queries d * 128 to (d + 1) * 128 - 1.
All inputs are finite; a program needn't handle non-finite values.
Results may differ from the reference program's by a relative error of at most 0.00097.
Values may be sent and summed in bfloat16 or wider, within the bound.
No kernel may reach another device: no remote copies, remote signals or barrier semaphores. Data moves between devices by JAX's collectives and lax.ppermute only.
A program may use at most 64 MiB of HBM per device.

```python
import math
import jax
import jax.numpy as jnp
from jax import lax

CLASSES = 64
TILE = 512
BR = 4
BC = 8
KT = 8
SEED_DEV = 32
ITERS = 2
QDEV = 128
QUERIES = 65536
URLS = 65536
TILES = 4096
SEEDS = 16384
N_COL = 16
DEVICES = 512


def draw_tile_coords(key, part):
    key = jax.random.fold_in(key, 1)
    keys = jax.random.split(key, DEVICES)
    orders = jax.vmap(lambda k: jax.random.permutation(k, BR * BC))(keys)[:, :KT]
    places = orders.reshape(TILES).astype(jnp.int32)
    return jnp.stack([places // BC, places % BC], axis=1).astype(jnp.int32)


def draw_tile_count(key, part):
    key = jax.random.fold_in(key, 2)
    first, second, third = jax.random.split(key, 3)
    upper = jax.random.randint(first, (DEVICES,), 1, KT + 1)
    lower = jax.random.randint(second, (DEVICES,), 1, KT + 1)
    counts = jnp.minimum(upper, lower)
    chosen = jax.random.randint(third, (), 0, DEVICES)
    return counts.at[chosen].set(KT).astype(jnp.int32)


def draw_seed_ids(key, part):
    key = jax.random.fold_in(key, 3)
    offsets = jnp.repeat(jnp.arange(DEVICES, dtype=jnp.int32) * QDEV, SEED_DEV)
    inside = jax.random.randint(key, (SEEDS,), 0, QDEV)
    values = offsets + inside
    values = values.at[0].set(0).at[SEEDS - 1].set(QUERIES - 1)
    return values.astype(jnp.int32)


def draw_click_tiles(key, part):
    key = jax.random.fold_in(key, 4)
    pick_key, size_key = jax.random.split(key, 2)
    shape = (TILES, TILE, TILE)
    present = jax.random.randint(pick_key, shape, 0, 16) == 0
    level = 1.0 - jax.random.uniform(size_key, shape, jnp.float32)
    values = 0.05 * jnp.exp(-jnp.log(level) / 1.2)
    values = jnp.minimum(values, 20.0)
    return jnp.where(present, values, 0.0).astype(jnp.bfloat16)


def draw_prior_labels(key, part):
    key = jax.random.fold_in(key, 5)
    first_key, second_key, both_key, base_key, peak_key = jax.random.split(key, 5)
    first = jax.random.randint(first_key, (QUERIES,), 0, CLASSES)
    second = (first + jax.random.randint(second_key, (QUERIES,), 1, CLASSES)) % CLASSES
    has_second = jax.random.randint(both_key, (QUERIES,), 0, 2).astype(jnp.float32)
    class_index = jnp.arange(CLASSES, dtype=jnp.int32)[:, None]
    base = jnp.exp(jax.random.uniform(base_key, (CLASSES, QUERIES), jnp.float32, math.log(0.01), math.log(0.1)))
    peaks = jnp.exp(jax.random.uniform(peak_key, (2, QUERIES), jnp.float32, 0.0, math.log(9.9)))
    first_part = peaks[0][None, :] * (class_index == first[None, :]).astype(jnp.float32)
    second_part = (peaks[1] * has_second)[None, :] * (class_index == second[None, :]).astype(jnp.float32)
    return (base + first_part + second_part).astype(jnp.float32)


def plant(result, own_key, least, high):
    shape = result.shape
    spot = [jax.random.randint(jax.random.fold_in(own_key, axis), (), 0, shape[axis]) for axis in range(len(shape))]
    result = result.at[tuple(spot)].set(least)
    longest = shape.index(max(shape))
    spot[longest] = (spot[longest] + 1) % shape[longest]
    return result.at[tuple(spot)].set(high)


def setup_inputs(seed: int = 0) -> dict:
    arg_keys = jax.random.split(jax.random.key(seed), 7)
    return {
        "click_tiles": draw_click_tiles(jax.random.fold_in(arg_keys[6], 71), 0),
        "tile_coords": draw_tile_coords(jax.random.fold_in(arg_keys[6], 71), 0),
        "tile_count": draw_tile_count(jax.random.fold_in(arg_keys[6], 71), 0),
        "prior_labels": draw_prior_labels(jax.random.fold_in(arg_keys[6], 71), 0),
        "seed_ids": draw_seed_ids(jax.random.fold_in(arg_keys[6], 71), 0),
        "seed_class": plant(jax.random.randint(arg_keys[5], (SEEDS,), 0, CLASSES), jax.random.fold_in(arg_keys[5], 1), 0, CLASSES - 1).astype(jnp.int32),
    }


blend_rate = 0.25
seed_weight = 8.0


def reference(click_tiles, tile_coords, tile_count, prior_labels, seed_ids, seed_class):
    queries = prior_labels.shape[1]
    query_blocks = queries // TILE
    url_blocks = URLS // TILE
    positions = jnp.arange(TILES, dtype=jnp.int32)
    device = positions // KT
    within = positions % KT
    active = (within < tile_count[device]).astype(jnp.float32)
    global_rows = ((device // N_COL) * BR + tile_coords[:, 0]).astype(jnp.int32)
    global_cols = ((device % N_COL) * BC + tile_coords[:, 1]).astype(jnp.int32)
    items = (click_tiles, global_rows, global_cols, active)

    def degree_step(carry, item):
        block, qrow, ucol, weight = item
        query_deg, url_deg = carry
        wide = block.astype(jnp.float32)
        query_deg = query_deg.at[qrow].add(weight * jnp.sum(wide, axis=1))
        url_deg = url_deg.at[ucol].add(weight * jnp.sum(wide, axis=0))
        return (query_deg, url_deg), None

    zero_q = jnp.zeros((query_blocks, TILE), jnp.float32)
    zero_u = jnp.zeros((url_blocks, TILE), jnp.float32)
    (query_deg, url_deg), _ = lax.scan(degree_step, (zero_q, zero_u), items)
    query_deg = query_deg.reshape(queries)
    url_deg = url_deg.reshape(URLS)
    seed_map = jnp.zeros((CLASSES, queries), jnp.float32).at[seed_class, seed_ids].add(1.0)

    labels = prior_labels
    url_labels = jnp.zeros((CLASSES, URLS), jnp.float32)
    for iteration in range(ITERS):
        query_rounded = labels.astype(jnp.bfloat16).reshape(CLASSES, query_blocks, TILE)

        def url_step(carry, item):
            block, qrow, ucol, weight = item
            piece = query_rounded[:, qrow, :]
            term = jnp.dot(piece, block, preferred_element_type=jnp.float32)
            return carry.at[:, ucol, :].add(weight * term), None

        url_sums, _ = lax.scan(url_step, jnp.zeros((CLASSES, url_blocks, TILE), jnp.float32), items)
        url_labels = url_sums.reshape(CLASSES, URLS) / (url_deg + 1.0)
        url_rounded = url_labels.astype(jnp.bfloat16).reshape(CLASSES, url_blocks, TILE)

        def query_step(carry, item):
            block, qrow, ucol, weight = item
            piece = url_rounded[:, ucol, :]
            term = jnp.dot(piece, block.T, preferred_element_type=jnp.float32)
            return carry.at[:, qrow, :].add(weight * term), None

        query_sums, _ = lax.scan(query_step, jnp.zeros((CLASSES, query_blocks, TILE), jnp.float32), items)
        spread = query_sums.reshape(CLASSES, queries) / (query_deg + 1.0)
        labels = (1.0 - blend_rate) * spread + blend_rate * seed_weight * seed_map
    return labels, url_labels
```

```python
import jax
import jax.numpy as jnp
from jax import lax
from jax.experimental import pallas as pl
from jax.experimental.pallas import tpu as pltpu
from jax.sharding import Mesh, PartitionSpec as P

BR = 4
BC = 8
ITERS = 2
LANES = 128
EXTRA = 16
SCALE = 512.0

blend_rate = 0.25
seed_weight = 8.0

CHIPS = ("xh", "y")
COL = ("xl", "z")


def url_kernel(slots, meta, labels, tiles, own, other):
    own[...] = jnp.zeros_like(own)
    other[...] = jnp.zeros_like(other)
    core = meta[2 * slots + 1]
    rows = own.shape[1]
    classes = labels.shape[1]
    for k in range(slots):

        @pl.when(k < meta[2 * slots])
        def _():
            a = meta[2 * k]
            b = meta[2 * k + 1]
            left = jnp.concatenate([labels[4 * a + i] for i in range(4)], axis=1)
            if rows > classes:
                left = jnp.concatenate([left, jnp.ones((rows - classes, left.shape[1]), left.dtype)], axis=0)
            for out, parity in ((other, 1 - core), (own, core)):
                near = pl.ds(pl.multiple_of(parity * LANES, LANES), LANES)
                far = pl.ds(pl.multiple_of((parity + 2) * LANES, LANES), LANES)
                right = jnp.concatenate([tiles[k, :, near], tiles[k, :, far]], axis=1)
                term = jnp.dot(left, right, preferred_element_type=jnp.float32)
                out[2 * b] += term[:, :LANES]
                out[2 * b + 1] += term[:, LANES:]


def query_kernel(slots, meta, own, other, tiles, sums):
    sums[...] = jnp.zeros_like(sums)
    core = meta[2 * slots + 1]
    rows = sums.shape[1]
    classes = own.shape[1]
    for k in range(slots):

        @pl.when(k < meta[2 * slots])
        def _():
            a = meta[2 * k]
            b = meta[2 * k + 1]
            term = None
            for labels, parity in ((own, core), (other, 1 - core)):
                near = pl.ds(pl.multiple_of(parity * LANES, LANES), LANES)
                far = pl.ds(pl.multiple_of((parity + 2) * LANES, LANES), LANES)
                left = jnp.concatenate([labels[2 * b], labels[2 * b + 1]], axis=1)
                if rows > classes:
                    left = jnp.concatenate([left, jnp.ones((rows - classes, left.shape[1]), left.dtype)], axis=0)
                right = jnp.concatenate([tiles[k, :, near], tiles[k, :, far]], axis=1)
                part = lax.dot_general(left, right, (((1,), (1,)), ((), ())), preferred_element_type=jnp.float32)
                term = part if term is None else term + part
            for i in range(4):
                sums[4 * a + i] += term[:, i * LANES : (i + 1) * LANES]


def local_call(kernel, meta, operands, out_shape):
    spec = pl.BlockSpec(memory_space=pltpu.VMEM)
    return pl.pallas_call(
        kernel,
        in_specs=[pl.BlockSpec(memory_space=pltpu.SMEM)] + [spec] * len(operands),
        out_specs=jax.tree.map(lambda _: spec, out_shape),
        out_shape=out_shape,
        compiler_params=pltpu.CompilerParams(vmem_limit_bytes=32 * 1024 * 1024),
        cost_estimate=pl.CostEstimate(flops=8 * 2 * 64 * 512 * 512, bytes_accessed=5 << 20, transcendentals=0),
    )(meta, *operands)


def inverse(degree):
    return jnp.where(degree > 0.0, SCALE / jnp.where(degree > 0.0, degree, 1.0), 0.0)


def degree_rows(degree):
    power = jnp.where(degree > 0.0, jnp.floor(jnp.log2(jnp.maximum(degree, 1e-30))), 0.0)
    part = degree * jnp.exp2(-power)
    high = part.astype(jnp.float16)
    low = (part - high.astype(jnp.float32)).astype(jnp.float16)
    return jnp.concatenate([power.astype(jnp.float16), high, low], axis=1)


def degree_of(rows):
    rows = rows.astype(jnp.float32)
    return (rows[:, 1:2] + rows[:, 2:3]) * jnp.exp2(rows[:, 0:1])


def exchange(pieces, axes):
    return lax.all_to_all(pieces, axes, 0, 0, tiled=True)


def spread(piece, axes):
    count = lax.axis_size(axes)
    return exchange(jnp.broadcast_to(piece[None], (count,) + piece.shape), axes)


def reduce(sums, classes, axes, known):
    if known is None:
        degree = sums[:, classes : classes + 1]
        scale = inverse(degree)
        message = jnp.concatenate([(sums[:, :classes] * scale).astype(jnp.float16), degree_rows(degree)], axis=1)
        arrived = exchange(message, axes)
        weights = degree_of(arrived[:, classes:])
        arrived = arrived[:, :classes]
        total = jnp.sum(weights, axis=0) + 1.0
        known = (scale, weights / SCALE, total)
    else:
        arrived = exchange((sums * known[0]).astype(jnp.float16), axes)
    shares = jnp.sum(arrived.astype(jnp.float32) * known[1], axis=0)
    return shares / known[2], known


def shards(click_tiles, tile_coords, tile_count, prior_labels, seed_ids, seed_class):
    slots, tile_size = (click_tiles.shape[0], click_tiles.shape[1])
    classes, query_local = prior_labels.shape
    col_count = lax.axis_size(COL)
    chip_count = lax.axis_size(CHIPS)
    core = lax.axis_index("core").astype(jnp.int32)
    meta = jnp.concatenate([tile_coords.reshape(-1), tile_count, core[None]])

    offset = lax.axis_index(CHIPS + ("core",) + COL) * query_local
    class_onehot = (seed_class[None, :] == jnp.arange(classes)[:, None]).astype(jnp.bfloat16)
    place_onehot = ((seed_ids - offset)[:, None] == jnp.arange(query_local)[None, :]).astype(jnp.bfloat16)
    seed_map = jnp.dot(class_onehot, place_onehot, preferred_element_type=jnp.float32)
    seeds = blend_rate * seed_weight * seed_map

    labels = prior_labels
    url_known = query_known = None
    for iteration in range(ITERS):
        rows = classes + (EXTRA if iteration == 0 else 0)
        gathered = spread(labels.astype(jnp.bfloat16), COL)
        piece = jax.ShapeDtypeStruct((chip_count, rows, LANES), jnp.float32)
        own, other = local_call(
            lambda *refs: url_kernel(slots, *refs), meta, (gathered, click_tiles), (piece, piece)
        )
        if rows > classes:
            own, other = own[:, : classes + 8], other[:, : classes + 8]
        both = own + lax.ppermute(other, "core", [(0, 1), (1, 0)])
        url_labels, url_known = reduce(both, classes, CHIPS, url_known)
        own = spread(url_labels.astype(jnp.bfloat16), CHIPS)
        other = lax.ppermute(own, "core", [(0, 1), (1, 0)])
        sums = local_call(
            lambda *refs: query_kernel(slots, *refs),
            meta,
            (own, other, click_tiles),
            jax.ShapeDtypeStruct((col_count, rows, LANES), jnp.float32),
        )
        mean, query_known = reduce(sums, classes, COL, query_known)
        labels = (1.0 - blend_rate) * mean + seeds
    return labels, url_labels


def solution(mesh):
    grid = Mesh(mesh.devices.reshape(2, 8, 2, 2, 8), ("xh", "y", "core", "xl", "z"))
    row = ("xh", "y", "core")
    everywhere = row + COL
    placed = (
        P(everywhere, None, None),
        P(everywhere, None),
        P(everywhere),
        P(None, everywhere),
        P(everywhere),
        P(everywhere),
    )
    return jax.shard_map(
        shards,
        mesh=grid,
        in_specs=placed,
        out_specs=(P(None, everywhere), P(None, COL + row)),
        check_vma=False,
    )
```

```python
import jax
import jax.numpy as jnp
from jax import lax
from jax.experimental import pallas as pl
from jax.experimental.pallas import tpu as pltpu
from jax.sharding import Mesh, PartitionSpec as P

BR = 4
BC = 8
ITERS = 2
LANES = 128
EXTRA = 16
SCALE = 512.0
VMEM_LIMIT = 16 * 1024 * 1024

blend_rate = 0.25
seed_weight = 8.0

CHIPS = ("xh", "y")
COL = ("xl", "z")


def load_kernel(source, loaded, sem):
    copy = pltpu.make_async_copy(source, loaded, sem)
    copy.start()
    copy.wait()


def widened(labels, rows, live):
    if rows > labels.shape[0]:
        ones = jnp.ones((rows - labels.shape[0], labels.shape[1]), labels.dtype)
        labels = jnp.concatenate([labels, ones], axis=0)
    return labels * live


def live_slot(slots, meta, k):
    return (k < meta[2 * slots]).astype(jnp.float32).astype(jnp.bfloat16)


def url_kernel(slots, meta, labels, tiles, own, other, kept):
    own[...] = jnp.zeros_like(own)
    other[...] = jnp.zeros_like(other)
    first = meta[2 * slots + 1] == 0
    for k in range(slots):
        a = meta[2 * k]
        b = meta[2 * k + 1]
        left = jnp.concatenate([labels[4 * a + i] for i in range(4)], axis=1)
        left = widened(left, own.shape[1], live_slot(slots, meta, k))
        term = jnp.dot(left, tiles[k], preferred_element_type=jnp.float32)
        for i in range(2):
            even = term[:, 2 * i * LANES : (2 * i + 1) * LANES]
            odd = term[:, (2 * i + 1) * LANES : (2 * i + 2) * LANES]
            own[2 * b + i] += jnp.where(first, even, odd)
            other[2 * b + i] += jnp.where(first, odd, even)


def query_kernel(slots, meta, labels, tiles, sums, kept):
    sums[...] = jnp.zeros_like(sums)
    for k in range(slots):
        a = meta[2 * k]
        b = meta[2 * k + 1]
        left = jnp.concatenate([labels[j % 2, 2 * b + j // 2] for j in range(4)], axis=1)
        left = widened(left, sums.shape[1], live_slot(slots, meta, k))
        term = lax.dot_general(left, tiles[k], (((1,), (1,)), ((), ())), preferred_element_type=jnp.float32)
        for i in range(4):
            sums[4 * a + i] += term[:, i * LANES : (i + 1) * LANES]


def local_call(kernel, meta, labels, tiles, shapes):
    slots = tiles.shape[0]
    spec = pl.BlockSpec(memory_space=pltpu.VMEM)
    sums = tuple(jax.ShapeDtypeStruct(shape, jnp.float32) for shape in shapes)
    return pl.pallas_call(
        lambda *refs: kernel(slots, *refs),
        in_specs=[pl.BlockSpec(memory_space=pltpu.SMEM), spec, spec],
        out_specs=(spec,) * (len(sums) + 1),
        out_shape=sums + (pltpu.VMEM(tiles.shape, tiles.dtype),),
        input_output_aliases={2: len(sums)},
        compiler_params=pltpu.CompilerParams(vmem_limit_bytes=VMEM_LIMIT),
        cost_estimate=pl.CostEstimate(flops=2 * 64 * 512 * 512 * 8, bytes_accessed=1 << 20, transcendentals=0),
    )(meta, labels, tiles)


def load(tiles):
    return pl.pallas_call(
        load_kernel,
        in_specs=[pl.BlockSpec(memory_space=pltpu.HBM)],
        out_specs=pl.BlockSpec(memory_space=pltpu.VMEM),
        out_shape=pltpu.VMEM(tiles.shape, tiles.dtype),
        scratch_shapes=[pltpu.SemaphoreType.DMA],
        compiler_params=pltpu.CompilerParams(vmem_limit_bytes=VMEM_LIMIT),
        cost_estimate=pl.CostEstimate(flops=0, bytes_accessed=4 << 20, transcendentals=0),
    )(tiles)


def inverse(degree):
    return jnp.where(degree > 0.0, SCALE / jnp.where(degree > 0.0, degree, 1.0), 0.0)


def degree_rows(degree):
    power = jnp.where(degree > 0.0, jnp.floor(jnp.log2(jnp.maximum(degree, 1e-30))), 0.0)
    part = degree * jnp.exp2(-power)
    high = part.astype(jnp.float16)
    low = (part - high.astype(jnp.float32)).astype(jnp.float16)
    return jnp.concatenate([power.astype(jnp.float16), high, low], axis=1)


def degree_of(rows):
    rows = rows.astype(jnp.float32)
    return (rows[:, 1:2] + rows[:, 2:3]) * jnp.exp2(rows[:, 0:1])


def exchange(pieces, axes):
    return lax.all_to_all(pieces, axes, 0, 0, tiled=True)


def spread(piece, axes):
    count = lax.axis_size(axes)
    return exchange(jnp.broadcast_to(piece[None], (count,) + piece.shape).astype(jnp.bfloat16), axes)


def partner(piece, first):
    both = lax.all_gather(piece, "core")
    return jnp.where(first, both[1], both[0])


def joined(own, other, classes, first, known):
    if known is None:
        degree = other[:, classes : classes + 1]
        scale = inverse(degree)
        rest = degree_rows(degree)
        rest = jnp.pad(rest, ((0, 0), (0, EXTRA - rest.shape[1]), (0, 0)))
        arrived = partner(jnp.concatenate([(other[:, :classes] * scale).astype(jnp.float16), rest], axis=1), first)
        degree = degree_of(arrived[:, classes:])
        weights = degree / SCALE
        shares = arrived[:, :classes].astype(jnp.float32) * weights
        come = jnp.concatenate([shares, degree], axis=1)
        return own[:, : classes + 1] + come, (scale, weights)
    arrived = partner((other * known[0]).astype(jnp.float16), first)
    return own + arrived.astype(jnp.float32) * known[1], known


def reduce(sums, classes, axes, known):
    if known is None:
        degree = sums[:, classes : classes + 1]
        scale = inverse(degree)
        message = jnp.concatenate([(sums[:, :classes] * scale).astype(jnp.float16), degree_rows(degree)], axis=1)
        arrived = exchange(message, axes)
        weights = degree_of(arrived[:, classes:])
        arrived = arrived[:, :classes]
        total = jnp.sum(weights, axis=0) + 1.0
        known = (scale, weights / SCALE, total)
    else:
        arrived = exchange((sums * known[0]).astype(jnp.float16), axes)
    shares = jnp.sum(arrived.astype(jnp.float32) * known[1], axis=0)
    return shares / known[2], known


def shards(click_tiles, tile_coords, tile_count, prior_labels, seed_ids, seed_class):
    slots, tile_size = (click_tiles.shape[0], click_tiles.shape[1])
    classes, query_local = prior_labels.shape
    col_count = lax.axis_size(COL)
    chip_count = lax.axis_size(CHIPS)
    core = lax.axis_index("core").astype(jnp.int32)
    meta = jnp.concatenate([tile_coords.reshape(-1), tile_count, core[None]])

    offset = lax.axis_index(CHIPS + ("core",) + COL) * query_local
    class_onehot = (seed_class[None, :] == jnp.arange(classes)[:, None]).astype(jnp.bfloat16)
    place_onehot = ((seed_ids - offset)[:, None] == jnp.arange(query_local)[None, :]).astype(jnp.bfloat16)
    seed_map = jnp.dot(class_onehot, place_onehot, preferred_element_type=jnp.float32)
    seeds = blend_rate * seed_weight * seed_map

    gathered = spread(prior_labels, COL)
    tiles = load(click_tiles)
    gathered, tiles, meta, seeds = lax.optimization_barrier((gathered, tiles, meta, seeds))
    core_known = url_known = query_known = None
    for iteration in range(ITERS):
        rows = classes + (EXTRA if iteration == 0 else 0)
        if iteration > 0:
            gathered = spread(labels.astype(jnp.bfloat16), COL)
        shape = (chip_count, rows, LANES)
        own, other, tiles = local_call(url_kernel, meta, gathered, tiles, (shape, shape))
        both, core_known = joined(own, other, classes, core == 0, core_known)
        url_labels, url_known = reduce(both, classes, CHIPS, url_known)
        both = lax.all_gather(spread(url_labels.astype(jnp.bfloat16), CHIPS), "core")
        sums, tiles = local_call(query_kernel, meta, both, tiles, ((col_count, rows, LANES),))
        mean, query_known = reduce(sums, classes, COL, query_known)
        labels = (1.0 - blend_rate) * mean + seeds
    return labels, url_labels


def solution(mesh):
    grid = Mesh(mesh.devices.reshape(2, 8, 2, 2, 8), ("xh", "y", "core", "xl", "z"))
    row = ("xh", "y", "core")
    everywhere = row + COL
    placed = (
        P(everywhere, None, None),
        P(everywhere, None),
        P(everywhere),
        P(None, everywhere),
        P(everywhere),
        P(everywhere),
    )
    return jax.shard_map(
        shards,
        mesh=grid,
        in_specs=placed,
        out_specs=(P(None, everywhere), P(None, COL + row)),
        check_vma=False,
    )
```

```python
import jax
import jax.numpy as jnp
from jax import lax
from jax.experimental import pallas as pl
from jax.experimental.pallas import tpu as pltpu
from jax.sharding import Mesh, PartitionSpec as P

BR = 4
BC = 8
ITERS = 2
LANES = 128
EXTRA = 16
SCALE = 512.0
VMEM_LIMIT = 16 * 1024 * 1024

blend_rate = 0.25
seed_weight = 8.0

CHIPS = ("xh", "y")
COL = ("xl", "z")


def load_kernel(source, loaded, sem):
    copy = pltpu.make_async_copy(source, loaded, sem)
    copy.start()
    copy.wait()


def widened(labels, rows, live):
    if rows > labels.shape[0]:
        ones = jnp.ones((rows - labels.shape[0], labels.shape[1]), labels.dtype)
        labels = jnp.concatenate([labels, ones], axis=0)
    return labels * live


def live_slot(slots, meta, k):
    return (k < meta[2 * slots]).astype(jnp.float32).astype(jnp.bfloat16)


def fetch(tiles, held, sem):
    copy = pltpu.make_async_copy(tiles, held, sem)
    copy.start()
    return copy


def url_kernel(slots, meta, labels, tiles, own, other, *refs):
    held, sem = refs[-2:]
    copy = fetch(tiles, held, sem)
    own[...] = jnp.zeros_like(own)
    other[...] = jnp.zeros_like(other)
    first = meta[2 * slots + 1] == 0
    copy.wait()
    for k in range(slots):
        a = meta[2 * k]
        b = meta[2 * k + 1]
        left = jnp.concatenate([labels[4 * a + i] for i in range(4)], axis=1)
        left = widened(left, own.shape[1], live_slot(slots, meta, k))
        term = jnp.dot(left, held[k], preferred_element_type=jnp.float32)
        for i in range(2):
            even = term[:, 2 * i * LANES : (2 * i + 1) * LANES]
            odd = term[:, (2 * i + 1) * LANES : (2 * i + 2) * LANES]
            own[2 * b + i] += jnp.where(first, even, odd)
            other[2 * b + i] += jnp.where(first, odd, even)


def query_kernel(slots, meta, labels, tiles, sums, *refs):
    held, sem = refs[-2:]
    copy = fetch(tiles, held, sem)
    sums[...] = jnp.zeros_like(sums)
    copy.wait()
    for k in range(slots):
        a = meta[2 * k]
        b = meta[2 * k + 1]
        left = jnp.concatenate([labels[j % 2, 2 * b + j // 2] for j in range(4)], axis=1)
        left = widened(left, sums.shape[1], live_slot(slots, meta, k))
        term = lax.dot_general(left, held[k], (((1,), (1,)), ((), ())), preferred_element_type=jnp.float32)
        for i in range(4):
            sums[4 * a + i] += term[:, i * LANES : (i + 1) * LANES]


def local_call(kernel, meta, labels, tiles, shapes, last=False):
    slots = tiles.shape[0]
    spec = pl.BlockSpec(memory_space=pltpu.VMEM)
    there = pl.BlockSpec(memory_space=pl.ANY)
    out_shape = tuple(jax.ShapeDtypeStruct(shape, jnp.float32) for shape in shapes)
    aliases = {} if last else {2: len(out_shape)}
    if not last:
        out_shape += (jax.ShapeDtypeStruct(tiles.shape, tiles.dtype),)
    return pl.pallas_call(
        lambda *refs: kernel(slots, *refs),
        in_specs=[pl.BlockSpec(memory_space=pltpu.SMEM), spec, there],
        out_specs=(spec,) * len(shapes) + (there,) * (len(out_shape) - len(shapes)),
        out_shape=out_shape,
        scratch_shapes=[pltpu.VMEM(tiles.shape, tiles.dtype), pltpu.SemaphoreType.DMA],
        input_output_aliases=aliases,
        compiler_params=pltpu.CompilerParams(vmem_limit_bytes=VMEM_LIMIT),
        cost_estimate=pl.CostEstimate(flops=2 * 64 * 512 * 512 * 8, bytes_accessed=1 << 20, transcendentals=0),
    )(meta, labels, tiles)


def load(tiles):
    return pl.pallas_call(
        load_kernel,
        in_specs=[pl.BlockSpec(memory_space=pltpu.HBM)],
        out_specs=pl.BlockSpec(memory_space=pltpu.VMEM),
        out_shape=jax.ShapeDtypeStruct(tiles.shape, tiles.dtype),
        scratch_shapes=[pltpu.SemaphoreType.DMA],
        compiler_params=pltpu.CompilerParams(vmem_limit_bytes=VMEM_LIMIT),
        cost_estimate=pl.CostEstimate(flops=0, bytes_accessed=4 << 20, transcendentals=0),
    )(tiles)


def inverse(degree):
    return jnp.where(degree > 0.0, SCALE / jnp.where(degree > 0.0, degree, 1.0), 0.0)


def degree_rows(degree):
    power = jnp.where(degree > 0.0, jnp.floor(jnp.log2(jnp.maximum(degree, 1e-30))), 0.0)
    part = degree * jnp.exp2(-power)
    high = part.astype(jnp.float16)
    low = (part - high.astype(jnp.float32)).astype(jnp.float16)
    return jnp.concatenate([power.astype(jnp.float16), high, low], axis=1)


def degree_of(rows):
    rows = rows.astype(jnp.float32)
    return (rows[:, 1:2] + rows[:, 2:3]) * jnp.exp2(rows[:, 0:1])


def exchange(pieces, axes):
    return lax.all_to_all(pieces, axes, 0, 0, tiled=True)


def spread(piece, axes):
    count = lax.axis_size(axes)
    return exchange(jnp.broadcast_to(piece[None], (count,) + piece.shape).astype(jnp.bfloat16), axes)


def partner(piece, first):
    both = lax.all_gather(piece, "core")
    return jnp.where(first, both[1], both[0])


def joined(own, other, classes, first, known):
    if known is None:
        degree = other[:, classes : classes + 1]
        scale = inverse(degree)
        rest = degree_rows(degree)
        rest = jnp.pad(rest, ((0, 0), (0, EXTRA - rest.shape[1]), (0, 0)))
        arrived = partner(jnp.concatenate([(other[:, :classes] * scale).astype(jnp.float16), rest], axis=1), first)
        degree = degree_of(arrived[:, classes:])
        weights = degree / SCALE
        shares = arrived[:, :classes].astype(jnp.float32) * weights
        come = jnp.concatenate([shares, degree], axis=1)
        return own[:, : classes + 1] + come, (scale, weights)
    arrived = partner((other * known[0]).astype(jnp.float16), first)
    return own + arrived.astype(jnp.float32) * known[1], known


def reduce(sums, classes, axes, known):
    if known is None:
        degree = sums[:, classes : classes + 1]
        scale = inverse(degree)
        message = jnp.concatenate([(sums[:, :classes] * scale).astype(jnp.float16), degree_rows(degree)], axis=1)
        arrived = exchange(message, axes)
        weights = degree_of(arrived[:, classes:])
        arrived = arrived[:, :classes]
        total = jnp.sum(weights, axis=0) + 1.0
        known = (scale, weights / SCALE, total)
    else:
        arrived = exchange((sums * known[0]).astype(jnp.float16), axes)
    shares = jnp.sum(arrived.astype(jnp.float32) * known[1], axis=0)
    return shares / known[2], known


def shards(click_tiles, tile_coords, tile_count, prior_labels, seed_ids, seed_class):
    slots, tile_size = (click_tiles.shape[0], click_tiles.shape[1])
    classes, query_local = prior_labels.shape
    col_count = lax.axis_size(COL)
    chip_count = lax.axis_size(CHIPS)
    core = lax.axis_index("core").astype(jnp.int32)
    meta = jnp.concatenate([tile_coords.reshape(-1), tile_count, core[None]])

    offset = lax.axis_index(CHIPS + ("core",) + COL) * query_local
    class_onehot = (seed_class[None, :] == jnp.arange(classes)[:, None]).astype(jnp.bfloat16)
    place_onehot = ((seed_ids - offset)[:, None] == jnp.arange(query_local)[None, :]).astype(jnp.bfloat16)
    seed_map = jnp.dot(class_onehot, place_onehot, preferred_element_type=jnp.float32)
    seeds = blend_rate * seed_weight * seed_map

    gathered = spread(prior_labels, COL)
    tiles = load(click_tiles)
    gathered, tiles, meta, seeds = lax.optimization_barrier((gathered, tiles, meta, seeds))
    core_known = url_known = query_known = None
    for iteration in range(ITERS):
        rows = classes + (EXTRA if iteration == 0 else 0)
        if iteration > 0:
            gathered = spread(labels.astype(jnp.bfloat16), COL)
        shape = (chip_count, rows, LANES)
        own, other, tiles = local_call(url_kernel, meta, gathered, tiles, (shape, shape))
        both, core_known = joined(own, other, classes, core == 0, core_known)
        url_labels, url_known = reduce(both, classes, CHIPS, url_known)
        both = lax.all_gather(spread(url_labels.astype(jnp.bfloat16), CHIPS), "core")
        last = iteration == ITERS - 1
        sums, *rest = local_call(query_kernel, meta, both, tiles, ((col_count, rows, LANES),), last)
        tiles = rest[0] if rest else tiles
        mean, query_known = reduce(sums, classes, COL, query_known)
        labels = (1.0 - blend_rate) * mean + seeds
    return labels, url_labels


def solution(mesh):
    grid = Mesh(mesh.devices.reshape(2, 8, 2, 2, 8), ("xh", "y", "core", "xl", "z"))
    row = ("xh", "y", "core")
    everywhere = row + COL
    placed = (
        P(everywhere, None, None),
        P(everywhere, None),
        P(everywhere),
        P(None, everywhere),
        P(everywhere),
        P(everywhere),
    )
    return jax.shard_map(
        shards,
        mesh=grid,
        in_specs=placed,
        out_specs=(P(None, everywhere), P(None, COL + row)),
        check_vma=False,
    )
```

```python
import jax
import jax.numpy as jnp
from jax import lax
from jax.experimental import pallas as pl
from jax.experimental.pallas import tpu as pltpu
from jax.sharding import Mesh, PartitionSpec as P

BR = 4
BC = 8
ITERS = 2
LANES = 128
EXTRA = 16
SCALE = 512.0
VMEM_LIMIT = 16 * 1024 * 1024

blend_rate = 0.25
seed_weight = 8.0

CHIPS = ("xh", "y")
COL = ("xl", "z")


def load_kernel(source, loaded, sem):
    copy = pltpu.make_async_copy(source, loaded, sem)
    copy.start()
    copy.wait()


def widened(labels, rows, live):
    if rows > labels.shape[0]:
        ones = jnp.ones((rows - labels.shape[0], labels.shape[1]), labels.dtype)
        labels = jnp.concatenate([labels, ones], axis=0)
    return labels * live


def live_slot(slots, meta, k):
    return (k < meta[2 * slots]).astype(jnp.float32).astype(jnp.bfloat16)


def fetch(tiles, held, sem):
    copy = pltpu.make_async_copy(tiles, held, sem)
    copy.start()
    return copy


def url_kernel(slots, meta, labels, tiles, own, other, *refs):
    held, sem = refs[-2:]
    copy = fetch(tiles, held, sem)
    own[...] = jnp.zeros_like(own)
    other[...] = jnp.zeros_like(other)
    first = meta[2 * slots + 1] == 0
    copy.wait()
    for k in range(slots):
        a = meta[2 * k]
        b = meta[2 * k + 1]
        left = jnp.concatenate([labels[4 * a + i] for i in range(4)], axis=1)
        left = widened(left, own.shape[1], live_slot(slots, meta, k))
        term = jnp.dot(left, held[k], preferred_element_type=jnp.float32)
        for i in range(2):
            even = term[:, 2 * i * LANES : (2 * i + 1) * LANES]
            odd = term[:, (2 * i + 1) * LANES : (2 * i + 2) * LANES]
            own[2 * b + i] += jnp.where(first, even, odd)
            other[2 * b + i] += jnp.where(first, odd, even)


def query_kernel(slots, meta, labels, tiles, sums, *refs):
    held, sem = refs[-2:]
    copy = fetch(tiles, held, sem)
    sums[...] = jnp.zeros_like(sums)
    copy.wait()
    query_sums(slots, meta, labels, held, sums)


def last_kernel(slots, meta, labels, tiles, scores, sums, result, sem):
    copy = pltpu.make_async_copy(scores, result, sem)
    copy.start()
    sums[...] = jnp.zeros_like(sums)
    query_sums(slots, meta, labels, tiles, sums)
    copy.wait()


def query_sums(slots, meta, labels, held, sums):
    for k in range(slots):
        a = meta[2 * k]
        b = meta[2 * k + 1]
        left = jnp.concatenate([labels[j % 2, 2 * b + j // 2] for j in range(4)], axis=1)
        left = widened(left, sums.shape[1], live_slot(slots, meta, k))
        term = lax.dot_general(left, held[k], (((1,), (1,)), ((), ())), preferred_element_type=jnp.float32)
        for i in range(4):
            sums[4 * a + i] += term[:, i * LANES : (i + 1) * LANES]


COST = pl.CostEstimate(flops=2 * 64 * 512 * 512 * 8, bytes_accessed=1 << 20, transcendentals=0)


def local_call(kernel, meta, labels, tiles, shapes):
    slots = tiles.shape[0]
    spec = pl.BlockSpec(memory_space=pltpu.VMEM)
    there = pl.BlockSpec(memory_space=pl.ANY)
    sums = tuple(jax.ShapeDtypeStruct(shape, jnp.float32) for shape in shapes)
    return pl.pallas_call(
        lambda *refs: kernel(slots, *refs),
        in_specs=[pl.BlockSpec(memory_space=pltpu.SMEM), spec, there],
        out_specs=(spec,) * len(sums) + (there,),
        out_shape=sums + (jax.ShapeDtypeStruct(tiles.shape, tiles.dtype),),
        scratch_shapes=[pltpu.VMEM(tiles.shape, tiles.dtype), pltpu.SemaphoreType.DMA],
        input_output_aliases={2: len(sums)},
        compiler_params=pltpu.CompilerParams(vmem_limit_bytes=VMEM_LIMIT),
        cost_estimate=COST,
    )(meta, labels, tiles)


def last_call(meta, labels, tiles, scores, shape):
    slots = tiles.shape[0]
    spec = pl.BlockSpec(memory_space=pltpu.VMEM)
    return pl.pallas_call(
        lambda *refs: last_kernel(slots, *refs),
        in_specs=[pl.BlockSpec(memory_space=pltpu.SMEM), spec, spec, spec],
        out_specs=(spec, pl.BlockSpec(memory_space=pl.ANY)),
        out_shape=(
            jax.ShapeDtypeStruct(shape, jnp.float32),
            jax.ShapeDtypeStruct(scores.shape, scores.dtype),
        ),
        scratch_shapes=[pltpu.SemaphoreType.DMA],
        compiler_params=pltpu.CompilerParams(vmem_limit_bytes=VMEM_LIMIT),
        cost_estimate=COST,
    )(meta, labels, tiles, scores)


def load(tiles):
    return pl.pallas_call(
        load_kernel,
        in_specs=[pl.BlockSpec(memory_space=pltpu.HBM)],
        out_specs=pl.BlockSpec(memory_space=pltpu.VMEM),
        out_shape=jax.ShapeDtypeStruct(tiles.shape, tiles.dtype),
        scratch_shapes=[pltpu.SemaphoreType.DMA],
        compiler_params=pltpu.CompilerParams(vmem_limit_bytes=VMEM_LIMIT),
        cost_estimate=pl.CostEstimate(flops=0, bytes_accessed=4 << 20, transcendentals=0),
    )(tiles)


def inverse(degree):
    return jnp.where(degree > 0.0, SCALE / jnp.where(degree > 0.0, degree, 1.0), 0.0)


def degree_rows(degree):
    power = jnp.where(degree > 0.0, jnp.floor(jnp.log2(jnp.maximum(degree, 1e-30))), 0.0)
    part = degree * jnp.exp2(-power)
    high = part.astype(jnp.float16)
    low = (part - high.astype(jnp.float32)).astype(jnp.float16)
    return jnp.concatenate([power.astype(jnp.float16), high, low], axis=1)


def degree_of(rows):
    rows = rows.astype(jnp.float32)
    return (rows[:, 1:2] + rows[:, 2:3]) * jnp.exp2(rows[:, 0:1])


def exchange(pieces, axes):
    return lax.all_to_all(pieces, axes, 0, 0, tiled=True)


def spread(piece, axes):
    count = lax.axis_size(axes)
    return exchange(jnp.broadcast_to(piece[None], (count,) + piece.shape).astype(jnp.bfloat16), axes)


def partner(piece, first):
    both = lax.all_gather(piece, "core")
    return jnp.where(first, both[1], both[0])


def joined(own, other, classes, first, known):
    if known is None:
        degree = other[:, classes : classes + 1]
        scale = inverse(degree)
        rest = degree_rows(degree)
        rest = jnp.pad(rest, ((0, 0), (0, EXTRA - rest.shape[1]), (0, 0)))
        arrived = partner(jnp.concatenate([(other[:, :classes] * scale).astype(jnp.float16), rest], axis=1), first)
        degree = degree_of(arrived[:, classes:])
        weights = degree / SCALE
        shares = arrived[:, :classes].astype(jnp.float32) * weights
        come = jnp.concatenate([shares, degree], axis=1)
        return own[:, : classes + 1] + come, (scale, weights)
    arrived = partner((other * known[0]).astype(jnp.float16), first)
    return own + arrived.astype(jnp.float32) * known[1], known


def reduce(sums, classes, axes, known):
    if known is None:
        degree = sums[:, classes : classes + 1]
        scale = inverse(degree)
        message = jnp.concatenate([(sums[:, :classes] * scale).astype(jnp.float16), degree_rows(degree)], axis=1)
        arrived = exchange(message, axes)
        weights = degree_of(arrived[:, classes:])
        arrived = arrived[:, :classes]
        total = jnp.sum(weights, axis=0) + 1.0
        known = (scale, weights / SCALE, total)
    else:
        arrived = exchange((sums * known[0]).astype(jnp.float16), axes)
    shares = jnp.sum(arrived.astype(jnp.float32) * known[1], axis=0)
    return shares / known[2], known


def shards(click_tiles, tile_coords, tile_count, prior_labels, seed_ids, seed_class):
    slots, tile_size = (click_tiles.shape[0], click_tiles.shape[1])
    classes, query_local = prior_labels.shape
    col_count = lax.axis_size(COL)
    chip_count = lax.axis_size(CHIPS)
    core = lax.axis_index("core").astype(jnp.int32)
    meta = jnp.concatenate([tile_coords.reshape(-1), tile_count, core[None]])

    offset = lax.axis_index(CHIPS + ("core",) + COL) * query_local
    class_onehot = (seed_class[None, :] == jnp.arange(classes)[:, None]).astype(jnp.bfloat16)
    place_onehot = ((seed_ids - offset)[:, None] == jnp.arange(query_local)[None, :]).astype(jnp.bfloat16)
    seed_map = jnp.dot(class_onehot, place_onehot, preferred_element_type=jnp.float32)
    seeds = blend_rate * seed_weight * seed_map

    gathered = spread(prior_labels, COL)
    tiles = load(click_tiles)
    gathered, tiles, meta, seeds = lax.optimization_barrier((gathered, tiles, meta, seeds))
    core_known = url_known = query_known = None
    for iteration in range(ITERS):
        rows = classes + (EXTRA if iteration == 0 else 0)
        if iteration > 0:
            gathered = spread(labels.astype(jnp.bfloat16), COL)
        shape = (chip_count, rows, LANES)
        own, other, tiles = local_call(url_kernel, meta, gathered, tiles, (shape, shape))
        both, core_known = joined(own, other, classes, core == 0, core_known)
        url_labels, url_known = reduce(both, classes, CHIPS, url_known)
        both = lax.all_gather(spread(url_labels.astype(jnp.bfloat16), CHIPS), "core")
        shape = (col_count, rows, LANES)
        if iteration < ITERS - 1:
            sums, tiles = local_call(query_kernel, meta, both, tiles, (shape,))
        else:
            sums, url_labels = last_call(meta, both, tiles, url_labels, shape)
        mean, query_known = reduce(sums, classes, COL, query_known)
        labels = (1.0 - blend_rate) * mean + seeds
    return labels, url_labels


def solution(mesh):
    grid = Mesh(mesh.devices.reshape(2, 8, 2, 2, 8), ("xh", "y", "core", "xl", "z"))
    row = ("xh", "y", "core")
    everywhere = row + COL
    placed = (
        P(everywhere, None, None),
        P(everywhere, None),
        P(everywhere),
        P(None, everywhere),
        P(everywhere),
        P(everywhere),
    )
    return jax.shard_map(
        shards,
        mesh=grid,
        in_specs=placed,
        out_specs=(P(None, everywhere), P(None, COL + row)),
        check_vma=False,
    )
```

```python
import jax
import jax.numpy as jnp
from jax import lax
from jax.experimental import pallas as pl
from jax.experimental.pallas import tpu as pltpu
from jax.sharding import Mesh, PartitionSpec as P

BR = 4
BC = 8
ITERS = 2
LANES = 128
EXTRA = 16
SCALE = 512.0
VMEM_LIMIT = 16 * 1024 * 1024

blend_rate = 0.25
seed_weight = 8.0

CHIPS = ("xh", "y")
COL = ("xl", "z")


def widened(labels, rows, live):
    if rows > labels.shape[0]:
        ones = jnp.ones((rows - labels.shape[0], labels.shape[1]), labels.dtype)
        labels = jnp.concatenate([labels, ones], axis=0)
    return labels * live


def live_slot(slots, meta, k):
    return (k < meta[2 * slots]).astype(jnp.float32).astype(jnp.bfloat16)


def url_kernel(slots, meta, labels, tiles, own, other):
    own[...] = jnp.zeros_like(own)
    other[...] = jnp.zeros_like(other)
    first = meta[2 * slots + 1] == 0
    for k in range(slots):
        a = meta[2 * k]
        b = meta[2 * k + 1]
        left = jnp.concatenate([labels[4 * a + i] for i in range(4)], axis=1)
        left = widened(left, own.shape[1], live_slot(slots, meta, k))
        term = jnp.dot(left, tiles[k], preferred_element_type=jnp.float32)
        for i in range(2):
            even = term[:, 2 * i * LANES : (2 * i + 1) * LANES]
            odd = term[:, (2 * i + 1) * LANES : (2 * i + 2) * LANES]
            own[2 * b + i] += jnp.where(first, even, odd)
            other[2 * b + i] += jnp.where(first, odd, even)


def query_kernel(slots, meta, labels, tiles, sums):
    sums[...] = jnp.zeros_like(sums)
    for k in range(slots):
        a = meta[2 * k]
        b = meta[2 * k + 1]
        left = jnp.concatenate([labels[j % 2, 2 * b + j // 2] for j in range(4)], axis=1)
        left = widened(left, sums.shape[1], live_slot(slots, meta, k))
        term = lax.dot_general(left, tiles[k], (((1,), (1,)), ((), ())), preferred_element_type=jnp.float32)
        for i in range(4):
            sums[4 * a + i] += term[:, i * LANES : (i + 1) * LANES]


def last_kernel(slots, meta, labels, tiles, scores, sums, result, sem):
    copy = pltpu.make_async_copy(scores, result, sem)
    copy.start()
    query_kernel(slots, meta, labels, tiles, sums)
    copy.wait()


COST = pl.CostEstimate(flops=2 * 64 * 512 * 512 * 8, bytes_accessed=1 << 20, transcendentals=0)


def local_call(kernel, meta, labels, tiles, shapes):
    slots = tiles.shape[0]
    spec = pl.BlockSpec(memory_space=pltpu.VMEM)
    return pl.pallas_call(
        lambda *refs: kernel(slots, *refs),
        in_specs=[pl.BlockSpec(memory_space=pltpu.SMEM), spec, spec],
        out_specs=(spec,) * len(shapes),
        out_shape=tuple(jax.ShapeDtypeStruct(shape, jnp.float32) for shape in shapes),
        compiler_params=pltpu.CompilerParams(vmem_limit_bytes=VMEM_LIMIT),
        cost_estimate=COST,
    )(meta, labels, tiles)


def last_call(meta, labels, tiles, scores, shape):
    slots = tiles.shape[0]
    spec = pl.BlockSpec(memory_space=pltpu.VMEM)
    return pl.pallas_call(
        lambda *refs: last_kernel(slots, *refs),
        in_specs=[pl.BlockSpec(memory_space=pltpu.SMEM), spec, spec, spec],
        out_specs=(spec, pl.BlockSpec(memory_space=pl.ANY)),
        out_shape=(
            jax.ShapeDtypeStruct(shape, jnp.float32),
            jax.ShapeDtypeStruct(scores.shape, scores.dtype),
        ),
        scratch_shapes=[pltpu.SemaphoreType.DMA],
        compiler_params=pltpu.CompilerParams(vmem_limit_bytes=VMEM_LIMIT),
        cost_estimate=COST,
    )(meta, labels, tiles, scores)


def inverse(degree):
    return jnp.where(degree > 0.0, SCALE / jnp.where(degree > 0.0, degree, 1.0), 0.0)


def degree_rows(degree):
    power = jnp.where(degree > 0.0, jnp.floor(jnp.log2(jnp.maximum(degree, 1e-30))), 0.0)
    part = degree * jnp.exp2(-power)
    high = part.astype(jnp.float16)
    low = (part - high.astype(jnp.float32)).astype(jnp.float16)
    return jnp.concatenate([power.astype(jnp.float16), high, low], axis=1)


def degree_of(rows):
    rows = rows.astype(jnp.float32)
    return (rows[:, 1:2] + rows[:, 2:3]) * jnp.exp2(rows[:, 0:1])


def exchange(pieces, axes):
    return lax.all_to_all(pieces, axes, 0, 0, tiled=True)


def spread(piece, axes):
    count = lax.axis_size(axes)
    return exchange(jnp.broadcast_to(piece[None], (count,) + piece.shape).astype(jnp.bfloat16), axes)


def partner(piece, first):
    both = lax.all_gather(piece, "core")
    return jnp.where(first, both[1], both[0])


def joined(own, other, classes, first, known):
    if known is None:
        degree = other[:, classes : classes + 1]
        scale = inverse(degree)
        rest = degree_rows(degree)
        rest = jnp.pad(rest, ((0, 0), (0, EXTRA - rest.shape[1]), (0, 0)))
        arrived = partner(jnp.concatenate([(other[:, :classes] * scale).astype(jnp.float16), rest], axis=1), first)
        degree = degree_of(arrived[:, classes:])
        weights = degree / SCALE
        shares = arrived[:, :classes].astype(jnp.float32) * weights
        come = jnp.concatenate([shares, degree], axis=1)
        return own[:, : classes + 1] + come, (scale, weights)
    arrived = partner((other * known[0]).astype(jnp.float16), first)
    return own + arrived.astype(jnp.float32) * known[1], known


def reduce(sums, classes, axes, known):
    if known is None:
        degree = sums[:, classes : classes + 1]
        scale = inverse(degree)
        message = jnp.concatenate([(sums[:, :classes] * scale).astype(jnp.float16), degree_rows(degree)], axis=1)
        arrived = exchange(message, axes)
        weights = degree_of(arrived[:, classes:])
        arrived = arrived[:, :classes]
        total = jnp.sum(weights, axis=0) + 1.0
        known = (scale, weights / SCALE, total)
    else:
        arrived = exchange((sums * known[0]).astype(jnp.float16), axes)
    shares = jnp.sum(arrived.astype(jnp.float32) * known[1], axis=0)
    return shares / known[2], known


def shards(click_tiles, tile_coords, tile_count, prior_labels, seed_ids, seed_class):
    slots, tile_size = (click_tiles.shape[0], click_tiles.shape[1])
    classes, query_local = prior_labels.shape
    col_count = lax.axis_size(COL)
    chip_count = lax.axis_size(CHIPS)
    core = lax.axis_index("core").astype(jnp.int32)
    meta = jnp.concatenate([tile_coords.reshape(-1), tile_count, core[None]])

    offset = lax.axis_index(CHIPS + ("core",) + COL) * query_local
    class_onehot = (seed_class[None, :] == jnp.arange(classes)[:, None]).astype(jnp.bfloat16)
    place_onehot = ((seed_ids - offset)[:, None] == jnp.arange(query_local)[None, :]).astype(jnp.bfloat16)
    seed_map = jnp.dot(class_onehot, place_onehot, preferred_element_type=jnp.float32)
    seeds = blend_rate * seed_weight * seed_map

    gathered = spread(prior_labels, COL)
    gathered, meta, seeds = lax.optimization_barrier((gathered, meta, seeds))
    core_known = url_known = query_known = None
    for iteration in range(ITERS):
        rows = classes + (EXTRA if iteration == 0 else 0)
        if iteration > 0:
            gathered = spread(labels.astype(jnp.bfloat16), COL)
        shape = (chip_count, rows, LANES)
        own, other = local_call(url_kernel, meta, gathered, click_tiles, (shape, shape))
        both, core_known = joined(own, other, classes, core == 0, core_known)
        url_labels, url_known = reduce(both, classes, CHIPS, url_known)
        both = lax.all_gather(spread(url_labels.astype(jnp.bfloat16), CHIPS), "core")
        shape = (col_count, rows, LANES)
        if iteration < ITERS - 1:
            (sums,) = local_call(query_kernel, meta, both, click_tiles, (shape,))
        else:
            sums, url_labels = last_call(meta, both, click_tiles, url_labels, shape)
        mean, query_known = reduce(sums, classes, COL, query_known)
        labels = (1.0 - blend_rate) * mean + seeds
    return labels, url_labels


def solution(mesh):
    grid = Mesh(mesh.devices.reshape(2, 8, 2, 2, 8), ("xh", "y", "core", "xl", "z"))
    row = ("xh", "y", "core")
    everywhere = row + COL
    placed = (
        P(everywhere, None, None),
        P(everywhere, None),
        P(everywhere),
        P(None, everywhere),
        P(everywhere),
        P(everywhere),
    )
    return jax.shard_map(
        shards,
        mesh=grid,
        in_specs=placed,
        out_specs=(P(None, everywhere), P(None, COL + row)),
        check_vma=False,
    )
```

```python
import jax
import jax.numpy as jnp
from jax import lax
from jax.experimental import pallas as pl
from jax.experimental.pallas import tpu as pltpu
from jax.sharding import Mesh, PartitionSpec as P

BR = 4
BC = 8
ITERS = 2
LANES = 128
EXTRA = 16
SCALE = 512.0
LEAST = 1e-30
VMEM_LIMIT = 16 * 1024 * 1024

blend_rate = 0.25
seed_weight = 8.0

CHIPS = ("xh", "y")
COL = ("xl", "z")


def widened(labels, rows, live):
    if rows > labels.shape[0]:
        ones = jnp.ones((rows - labels.shape[0], labels.shape[1]), labels.dtype)
        labels = jnp.concatenate([labels, ones], axis=0)
    return labels * live


def live_slot(slots, meta, k):
    return (k < meta[2 * slots]).astype(jnp.float32).astype(jnp.bfloat16)


def url_kernel(slots, meta, labels, tiles, own, other):
    own[...] = jnp.zeros_like(own)
    other[...] = jnp.zeros_like(other)
    first = meta[2 * slots + 1] == 0
    for k in range(slots):
        a = meta[2 * k]
        b = meta[2 * k + 1]
        left = jnp.concatenate([labels[4 * a + i] for i in range(4)], axis=1)
        left = widened(left, own.shape[1], live_slot(slots, meta, k))
        term = jnp.dot(left, tiles[k], preferred_element_type=jnp.float32)
        for i in range(2):
            even = term[:, 2 * i * LANES : (2 * i + 1) * LANES]
            odd = term[:, (2 * i + 1) * LANES : (2 * i + 2) * LANES]
            own[2 * b + i] += jnp.where(first, even, odd)
            other[2 * b + i] += jnp.where(first, odd, even)


def query_kernel(slots, meta, labels, tiles, sums):
    sums[...] = jnp.zeros_like(sums)
    for k in range(slots):
        a = meta[2 * k]
        b = meta[2 * k + 1]
        left = jnp.concatenate([labels[j % 2, 2 * b + j // 2] for j in range(4)], axis=1)
        left = widened(left, sums.shape[1], live_slot(slots, meta, k))
        term = lax.dot_general(left, tiles[k], (((1,), (1,)), ((), ())), preferred_element_type=jnp.float32)
        for i in range(4):
            sums[4 * a + i] += term[:, i * LANES : (i + 1) * LANES]


def last_kernel(slots, meta, labels, tiles, scores, sums, result, sem):
    copy = pltpu.make_async_copy(scores, result, sem)
    copy.start()
    query_kernel(slots, meta, labels, tiles, sums)
    copy.wait()


COST = pl.CostEstimate(flops=2 * 64 * 512 * 512 * 8, bytes_accessed=1 << 20, transcendentals=0)


def local_call(kernel, meta, labels, tiles, shapes):
    slots = tiles.shape[0]
    spec = pl.BlockSpec(memory_space=pltpu.VMEM)
    return pl.pallas_call(
        lambda *refs: kernel(slots, *refs),
        in_specs=[pl.BlockSpec(memory_space=pltpu.SMEM), spec, spec],
        out_specs=(spec,) * len(shapes),
        out_shape=tuple(jax.ShapeDtypeStruct(shape, jnp.float32) for shape in shapes),
        compiler_params=pltpu.CompilerParams(vmem_limit_bytes=VMEM_LIMIT),
        cost_estimate=COST,
    )(meta, labels, tiles)


def last_call(meta, labels, tiles, scores, shape):
    slots = tiles.shape[0]
    spec = pl.BlockSpec(memory_space=pltpu.VMEM)
    return pl.pallas_call(
        lambda *refs: last_kernel(slots, *refs),
        in_specs=[pl.BlockSpec(memory_space=pltpu.SMEM), spec, spec, spec],
        out_specs=(spec, pl.BlockSpec(memory_space=pl.ANY)),
        out_shape=(
            jax.ShapeDtypeStruct(shape, jnp.float32),
            jax.ShapeDtypeStruct(scores.shape, scores.dtype),
        ),
        scratch_shapes=[pltpu.SemaphoreType.DMA],
        compiler_params=pltpu.CompilerParams(vmem_limit_bytes=VMEM_LIMIT),
        cost_estimate=COST,
    )(meta, labels, tiles, scores)


def degree_rows(degree):
    power = jnp.floor(jnp.log2(degree))
    part = degree * jnp.exp2(-power)
    high = part.astype(jnp.float16)
    low = (part - high.astype(jnp.float32)).astype(jnp.float16)
    return jnp.concatenate([power.astype(jnp.float16), high, low], axis=1)


def degree_of(rows):
    rows = rows.astype(jnp.float32)
    return (rows[:, 1:2] + rows[:, 2:3]) * jnp.exp2(rows[:, 0:1])


def exchange(pieces, axes):
    return lax.all_to_all(pieces, axes, 0, 0, tiled=True)


def spread(piece, axes):
    count = lax.axis_size(axes)
    return exchange(jnp.broadcast_to(piece[None], (count,) + piece.shape).astype(jnp.bfloat16), axes)


def partner(piece, first):
    both = lax.all_gather(piece, "core")
    return jnp.where(first, both[1], both[0])


def joined(own, other, classes, first, known):
    if known is None:
        degree = jnp.maximum(other[:, classes : classes + 1], LEAST)
        scale = SCALE / degree
        rest = degree_rows(degree)
        rest = jnp.pad(rest, ((0, 0), (0, EXTRA - rest.shape[1]), (0, 0)))
        arrived = partner(jnp.concatenate([(other[:, :classes] * scale).astype(jnp.float16), rest], axis=1), first)
        degree = degree_of(arrived[:, classes:])
        weights = degree / SCALE
        shares = arrived[:, :classes].astype(jnp.float32) * weights
        come = jnp.concatenate([shares, degree], axis=1)
        return own[:, : classes + 1] + come, (scale, weights)
    arrived = partner((other * known[0]).astype(jnp.float16), first)
    return own + arrived.astype(jnp.float32) * known[1], known


def reduce(sums, classes, axes, known):
    if known is None:
        degree = jnp.maximum(sums[:, classes : classes + 1], LEAST)
        scale = SCALE / degree
        message = jnp.concatenate([(sums[:, :classes] * scale).astype(jnp.float16), degree_rows(degree)], axis=1)
        arrived = exchange(message, axes)
        weights = degree_of(arrived[:, classes:])
        arrived = arrived[:, :classes]
        total = jnp.sum(weights, axis=0) + 1.0
        known = (scale, weights / SCALE, total)
    else:
        arrived = exchange((sums * known[0]).astype(jnp.float16), axes)
    shares = jnp.sum(arrived.astype(jnp.float32) * known[1], axis=0)
    return shares / known[2], known


def shards(click_tiles, tile_coords, tile_count, prior_labels, seed_ids, seed_class):
    slots, tile_size = (click_tiles.shape[0], click_tiles.shape[1])
    classes, query_local = prior_labels.shape
    col_count = lax.axis_size(COL)
    chip_count = lax.axis_size(CHIPS)
    core = lax.axis_index("core").astype(jnp.int32)
    meta = jnp.concatenate([tile_coords.reshape(-1), tile_count, core[None]])

    offset = lax.axis_index(CHIPS + ("core",) + COL) * query_local
    class_onehot = (seed_class[None, :] == jnp.arange(classes)[:, None]).astype(jnp.bfloat16)
    place_onehot = ((seed_ids - offset)[:, None] == jnp.arange(query_local)[None, :]).astype(jnp.bfloat16)
    seed_map = jnp.dot(class_onehot, place_onehot, preferred_element_type=jnp.float32)
    seeds = blend_rate * seed_weight * seed_map

    gathered = spread(prior_labels, COL)
    gathered, meta, seeds = lax.optimization_barrier((gathered, meta, seeds))
    core_known = url_known = query_known = None
    for iteration in range(ITERS):
        rows = classes + (EXTRA if iteration == 0 else 0)
        if iteration > 0:
            gathered = spread(labels.astype(jnp.bfloat16), COL)
        shape = (chip_count, rows, LANES)
        own, other = local_call(url_kernel, meta, gathered, click_tiles, (shape, shape))
        both, core_known = joined(own, other, classes, core == 0, core_known)
        url_labels, url_known = reduce(both, classes, CHIPS, url_known)
        both = lax.all_gather(spread(url_labels.astype(jnp.bfloat16), CHIPS), "core")
        shape = (col_count, rows, LANES)
        if iteration < ITERS - 1:
            (sums,) = local_call(query_kernel, meta, both, click_tiles, (shape,))
        else:
            sums, url_labels = last_call(meta, both, click_tiles, url_labels, shape)
        mean, query_known = reduce(sums, classes, COL, query_known)
        labels = (1.0 - blend_rate) * mean + seeds
    return labels, url_labels


def solution(mesh):
    grid = Mesh(mesh.devices.reshape(2, 8, 2, 2, 8), ("xh", "y", "core", "xl", "z"))
    row = ("xh", "y", "core")
    everywhere = row + COL
    placed = (
        P(everywhere, None, None),
        P(everywhere, None),
        P(everywhere),
        P(None, everywhere),
        P(everywhere),
        P(everywhere),
    )
    return jax.shard_map(
        shards,
        mesh=grid,
        in_specs=placed,
        out_specs=(P(None, everywhere), P(None, COL + row)),
        check_vma=False,
    )
```

```python
import jax
import jax.numpy as jnp
from jax import lax
from jax.experimental import pallas as pl
from jax.experimental.pallas import tpu as pltpu
from jax.sharding import Mesh, PartitionSpec as P

BR = 4
BC = 8
ITERS = 2
LANES = 128
EXTRA = 16
SCALE = 512.0
LEAST = 1e-30
VMEM_LIMIT = 16 * 1024 * 1024

blend_rate = 0.25
seed_weight = 8.0

CHIPS = ("xh", "y")
COL = ("xl", "z")


def widened(labels, rows, live):
    if rows > labels.shape[0]:
        ones = jnp.ones((rows - labels.shape[0], labels.shape[1]), labels.dtype)
        labels = jnp.concatenate([labels, ones], axis=0)
    return labels * live


def live_slot(slots, meta, k):
    return (k < meta[2 * slots]).astype(jnp.float32).astype(jnp.bfloat16)


def url_kernel(slots, meta, labels, tiles, own, other):
    own[...] = jnp.zeros_like(own)
    other[...] = jnp.zeros_like(other)
    first = meta[2 * slots + 1] == 0
    for k in range(slots):
        a = meta[2 * k]
        b = meta[2 * k + 1]
        left = jnp.concatenate([labels[4 * a + i] for i in range(4)], axis=1)
        left = widened(left, own.shape[1], live_slot(slots, meta, k))
        term = jnp.dot(left, tiles[k], preferred_element_type=jnp.float32)
        for i in range(2):
            even = term[:, 2 * i * LANES : (2 * i + 1) * LANES]
            odd = term[:, (2 * i + 1) * LANES : (2 * i + 2) * LANES]
            own[2 * b + i] += jnp.where(first, even, odd)
            other[2 * b + i] += jnp.where(first, odd, even)


def query_kernel(slots, meta, labels, tiles, sums):
    sums[...] = jnp.zeros_like(sums)
    for k in range(slots):
        a = meta[2 * k]
        b = meta[2 * k + 1]
        left = jnp.concatenate([labels[j % 2, 2 * b + j // 2] for j in range(4)], axis=1)
        left = widened(left, sums.shape[1], live_slot(slots, meta, k))
        term = lax.dot_general(left, tiles[k], (((1,), (1,)), ((), ())), preferred_element_type=jnp.float32)
        for i in range(4):
            sums[4 * a + i] += term[:, i * LANES : (i + 1) * LANES]


def last_kernel(slots, meta, labels, tiles, scores, sums, result, sem):
    copy = pltpu.make_async_copy(scores, result, sem)
    copy.start()
    query_kernel(slots, meta, labels, tiles, sums)
    copy.wait()


COST = pl.CostEstimate(flops=2 * 64 * 512 * 512 * 8, bytes_accessed=1 << 20, transcendentals=0)


def local_call(kernel, meta, labels, tiles, shapes):
    slots = tiles.shape[0]
    spec = pl.BlockSpec(memory_space=pltpu.VMEM)
    return pl.pallas_call(
        lambda *refs: kernel(slots, *refs),
        in_specs=[pl.BlockSpec(memory_space=pltpu.SMEM), spec, spec],
        out_specs=(spec,) * len(shapes),
        out_shape=tuple(jax.ShapeDtypeStruct(shape, jnp.float32) for shape in shapes),
        compiler_params=pltpu.CompilerParams(vmem_limit_bytes=VMEM_LIMIT),
        cost_estimate=COST,
    )(meta, labels, tiles)


def last_call(meta, labels, tiles, scores, shape):
    slots = tiles.shape[0]
    spec = pl.BlockSpec(memory_space=pltpu.VMEM)
    return pl.pallas_call(
        lambda *refs: last_kernel(slots, *refs),
        in_specs=[pl.BlockSpec(memory_space=pltpu.SMEM), spec, spec, spec],
        out_specs=(spec, pl.BlockSpec(memory_space=pl.ANY)),
        out_shape=(
            jax.ShapeDtypeStruct(shape, jnp.float32),
            jax.ShapeDtypeStruct(scores.shape, scores.dtype),
        ),
        scratch_shapes=[pltpu.SemaphoreType.DMA],
        compiler_params=pltpu.CompilerParams(vmem_limit_bytes=VMEM_LIMIT),
        cost_estimate=COST,
    )(meta, labels, tiles, scores)


def degree_rows(degree):
    power = jnp.floor(jnp.log2(degree))
    part = degree * jnp.exp2(-power)
    high = part.astype(jnp.float16)
    low = (part - high.astype(jnp.float32)).astype(jnp.float16)
    return jnp.concatenate([power.astype(jnp.float16), high, low], axis=1)


def degree_of(rows):
    rows = rows.astype(jnp.float32)
    return (rows[:, 1:2] + rows[:, 2:3]) * jnp.exp2(rows[:, 0:1])


def exchange(pieces, axes):
    return lax.all_to_all(pieces, axes, 0, 0, tiled=True)


def spread(piece, axes):
    count = lax.axis_size(axes)
    return exchange(jnp.broadcast_to(piece[None], (count,) + piece.shape).astype(jnp.bfloat16), axes)


def partner(piece, first):
    both = lax.all_gather(piece, "core")
    return jnp.where(first, both[1], both[0])


def joined(own, other, classes, first, known):
    if known is None:
        degree = jnp.maximum(other[:, classes : classes + 1], LEAST)
        scale = SCALE / degree
        rest = degree_rows(degree)
        rest = jnp.pad(rest, ((0, 0), (0, EXTRA - rest.shape[1]), (0, 0)))
        arrived = partner(jnp.concatenate([(other[:, :classes] * scale).astype(jnp.float16), rest], axis=1), first)
        degree = degree_of(arrived[:, classes:])
        weights = degree / SCALE
        shares = arrived[:, :classes].astype(jnp.float32) * weights
        come = jnp.concatenate([shares, degree], axis=1)
        return own[:, : classes + 1] + come, (scale, weights)
    arrived = partner((other * known[0]).astype(jnp.float16), first)
    return own + arrived.astype(jnp.float32) * known[1], known


def reduce(sums, classes, axes, known):
    if known is None:
        degree = jnp.maximum(sums[:, classes : classes + 1], LEAST)
        scale = SCALE / degree
        message = jnp.concatenate([(sums[:, :classes] * scale).astype(jnp.float16), degree_rows(degree)], axis=1)
        arrived = exchange(message, axes)
        weights = degree_of(arrived[:, classes:])
        arrived = arrived[:, :classes]
        total = jnp.sum(weights, axis=0) + 1.0
        known = (scale, weights / SCALE, total)
    else:
        arrived = exchange((sums * known[0]).astype(jnp.float16), axes)
    shares = jnp.sum(arrived.astype(jnp.float32) * known[1], axis=0)
    return shares / known[2], known


def shards(click_tiles, tile_coords, tile_count, prior_labels, seed_ids, seed_class):
    slots, tile_size = (click_tiles.shape[0], click_tiles.shape[1])
    classes, query_local = prior_labels.shape
    col_count = lax.axis_size(COL)
    chip_count = lax.axis_size(CHIPS)
    core = lax.axis_index("core").astype(jnp.int32)
    meta = jnp.concatenate([tile_coords.reshape(-1), tile_count, core[None]])

    offset = lax.axis_index(CHIPS + ("core",) + COL) * query_local
    class_onehot = (seed_class[None, :] == jnp.arange(classes)[:, None]).astype(jnp.bfloat16)
    place_onehot = ((seed_ids - offset)[:, None] == jnp.arange(query_local)[None, :]).astype(jnp.bfloat16)
    seed_map = jnp.dot(class_onehot, place_onehot, preferred_element_type=jnp.float32)
    seeds = blend_rate * seed_weight * seed_map

    copies = jnp.arange(col_count)[:, None, None] - core < col_count
    gathered = exchange(jnp.where(copies, prior_labels[None], 0.0).astype(jnp.bfloat16), COL)
    gathered, meta, seeds = lax.optimization_barrier((gathered, meta, seeds))
    core_known = url_known = query_known = None
    for iteration in range(ITERS):
        rows = classes + (EXTRA if iteration == 0 else 0)
        if iteration > 0:
            gathered = spread(labels.astype(jnp.bfloat16), COL)
        shape = (chip_count, rows, LANES)
        own, other = local_call(url_kernel, meta, gathered, click_tiles, (shape, shape))
        both, core_known = joined(own, other, classes, core == 0, core_known)
        url_labels, url_known = reduce(both, classes, CHIPS, url_known)
        both = lax.all_gather(spread(url_labels.astype(jnp.bfloat16), CHIPS), "core")
        shape = (col_count, rows, LANES)
        if iteration < ITERS - 1:
            (sums,) = local_call(query_kernel, meta, both, click_tiles, (shape,))
        else:
            sums, url_labels = last_call(meta, both, click_tiles, url_labels, shape)
        mean, query_known = reduce(sums, classes, COL, query_known)
        labels = (1.0 - blend_rate) * mean + seeds
    return labels, url_labels


def solution(mesh):
    grid = Mesh(mesh.devices.reshape(2, 8, 2, 2, 8), ("xh", "y", "core", "xl", "z"))
    row = ("xh", "y", "core")
    everywhere = row + COL
    placed = (
        P(everywhere, None, None),
        P(everywhere, None),
        P(everywhere),
        P(None, everywhere),
        P(everywhere),
        P(everywhere),
    )
    return jax.shard_map(
        shards,
        mesh=grid,
        in_specs=placed,
        out_specs=(P(None, everywhere), P(None, COL + row)),
        check_vma=False,
    )
```
